256 devices in a mesh: adapter: 32 (over y, x, core), tensor: 8 (over z).
Axes of the slice: x: 4, y: 4, z: 8, core: 2. Of those that a mesh axis runs over, the one named last changes fastest.
Arguments:
- attended: bfloat16 [4096, 8192], P('adapter'), may hold values from -6 to 6
- residual: bfloat16 [4096, 8192], P('adapter', 'tensor'), may hold values from -6 to 6
- output_matrix: bfloat16 [8192, 8192], P('adapter', 'tensor'), may hold values from -0.0625 to 0.0625
- adapter_down_weight: bfloat16 [512, 64, 8192], P('adapter', None, 'tensor'), may hold values from -0.0625 to 0.0625
- adapter_up_weight: bfloat16 [512, 64, 8192], P('adapter', None, 'tensor'), may hold values from -0.75 to 0.75
- request_adapter_index: int32 [4096], P('adapter'), may hold values from 0 to 511, as said below
Outputs:
- layer_out: bfloat16 [4096, 8192], P('adapter', 'tensor')
The draws below stay inside these ranges and needn't reach their ends.
Inputs may be any that keep to these rules, and one draw needn't show every extreme that they name: `request_adapter_index`: the owner of adapter id is id // 16. Among the 128 requests of one index of adapter, at most 16 use adapters of one owner, and exactly 16 use adapters of one common owner, the same for every index.
All inputs are finite; a program needn't handle non-finite values.
Results may differ from the reference program's by a relative error of at most 0.0052.
Values may be sent and summed in bfloat16 or wider, within the bound.
A program may use at most 128 MiB of HBM per device.

```python
import jax
import jax.numpy as jnp
from jax import lax

MODEL_WIDTH = 8192
ADAPTER_RANK = 64
REQ_DEV = 128
ADP_DEV = 16
CAP = 16
REQ = 4096
ADAPTER_TOTAL = 512


def draw_request_adapter_index(key, part):
    key = jax.random.fold_in(key, 7)
    blocks = REQ // REQ_DEV
    hot_key, rest_key = jax.random.split(key)
    hot = jax.random.randint(hot_key, (), 0, blocks).astype(jnp.int32)
    keys = jax.random.split(rest_key, blocks)

    def one_block(block_key):
        first, second, third = jax.random.split(block_key, 3)
        others = (hot + 1 + jnp.arange((blocks - 1) * CAP, dtype=jnp.int32) // CAP) % blocks
        others = jax.random.permutation(first, others)[:REQ_DEV - CAP]
        owners = jnp.concatenate([jnp.full((CAP,), hot, dtype=jnp.int32), others])
        owners = jax.random.permutation(second, owners)
        chosen = jax.random.randint(third, (REQ_DEV,), 0, ADP_DEV).astype(jnp.int32)
        return owners * ADP_DEV + chosen
    return jax.vmap(one_block)(keys).reshape(REQ).astype(jnp.int32)


def steps_of(key, extent, cuts, least, largest):
    factor_of = 1.0
    for axis_at, shards_of in cuts:
        draws = jax.random.uniform(jax.random.fold_in(jax.random.fold_in(key, 6), axis_at), (shards_of,), jnp.float32, least / len(cuts), largest / len(cuts))
        factor_of = factor_of * jnp.repeat(jnp.exp(draws), extent[axis_at] // shards_of).reshape((-1,) + (1,) * (len(extent) - 1 - axis_at))
    return factor_of


def scatter_about(own_key, extent, spread, bound, cuts=(), kind=jnp.bfloat16):
    result = jax.random.normal(own_key, extent, jnp.float32) * spread
    if len(cuts) > 0:
        result = steps_of(own_key, extent, cuts, -0.22, 0.18) * result
    return jnp.clip(result, min=-bound, max=bound).astype(kind)


def setup_inputs(seed: int = 0) -> dict:
    splits = jax.random.split(jax.random.key(seed), 7)
    return {
        "attended": scatter_about(splits[0], (REQ, MODEL_WIDTH), 1.0, 6.0, ((0, 32),)),
        "residual": scatter_about(splits[1], (REQ, MODEL_WIDTH), 1.0, 6.0, ((0, 32), (1, 8))),
        "output_matrix": scatter_about(splits[2], (MODEL_WIDTH, MODEL_WIDTH), MODEL_WIDTH ** -0.5, 0.0625, ((0, 32), (1, 8))),
        "adapter_down_weight": scatter_about(splits[3], (ADAPTER_TOTAL, ADAPTER_RANK, MODEL_WIDTH), MODEL_WIDTH ** -0.5, 0.0625, ((0, 32), (2, 8))),
        "adapter_up_weight": scatter_about(splits[4], (ADAPTER_TOTAL, ADAPTER_RANK, MODEL_WIDTH), ADAPTER_RANK ** -0.5, 0.75, ((0, 32), (2, 8))),
        "request_adapter_index": draw_request_adapter_index(jax.random.fold_in(splits[6], 71), 0),
    }


adapter_scale = 2.0


def reference(attended, residual, output_matrix, adapter_down_weight, adapter_up_weight, request_adapter_index):
    base = jnp.dot(attended, output_matrix, preferred_element_type=jnp.float32)
    blocks_x = attended.reshape(-1, REQ_DEV, MODEL_WIDTH)
    blocks_id = request_adapter_index.reshape(-1, REQ_DEV)

    def one_block(pair):
        rows, selected_adapters = pair
        down_projected = jnp.take(adapter_down_weight, selected_adapters, axis=0).astype(jnp.float32)
        lower_bound = jnp.einsum("rd,rkd->rk", rows.astype(jnp.float32), down_projected).astype(jnp.bfloat16)
        upper_bound = jnp.take(adapter_up_weight, selected_adapters, axis=0).astype(jnp.float32)
        return (jnp.einsum("wm,wmn->wn", lower_bound.astype(jnp.float32), upper_bound) * adapter_scale).astype(jnp.bfloat16)

    lowrank_update = lax.map(one_block, (blocks_x, blocks_id)).reshape(REQ, MODEL_WIDTH)
    total = residual.astype(jnp.float32) + base + lowrank_update.astype(jnp.float32)
    return total.astype(jnp.bfloat16)
```

```python
import functools

import jax
import jax.numpy as jnp
from jax import lax
from jax.experimental import pallas as pl
from jax.experimental.pallas import tpu as pltpu
from jax.sharding import PartitionSpec as P

adapter_scale = 2.0
NY, NX, NC = 4, 4, 2
GROUPS = NY * NX * NC
CAP = 16
META = 128
MESH = pl.DeviceIdType.MESH
f32, bf16, i32 = jnp.float32, jnp.bfloat16, jnp.int32


def iota(shape, dim):
    return lax.broadcasted_iota(i32, shape, dim)


def kernel(
    nz, idx_ref, att, res_hbm, w_hbm, down_hbm, up_hbm, out_ref,
    xz, res, down, up, fwd, got, low_own, low_in, low_sum, low_all, spread, delta, back,
    xb, wg, keep, sib_out, sib_in, sum_out, sum_in,
    load_sem, fs, fr, bs, br, ls, lr, gs, gr, xs, xr, es, er, ws, wr, ps, pr, rs, rr,
):
    me = lax.axis_index("adapter")
    z = lax.axis_index("tensor")
    core = lax.rem(me, NC)
    x = lax.rem(lax.div(me, NC), NX)
    y = lax.div(me, NC * NX)
    par = lax.rem(z, 2)
    rows, cols = out_ref.shape
    slots = GROUPS * CAP
    kcols = xb.shape[-1]
    quarter = rows // 4
    wblk = w_hbm.shape[0]

    def dev(yy, xx, cc):
        return (yy * NX + xx) * NC + cc

    def remote(src, dst, ssem, rsem, a, t):
        return pltpu.make_async_remote_copy(
            src_ref=src, dst_ref=dst, send_sem=ssem, recv_sem=rsem,
            device_id=(a, t), device_id_type=MESH)

    load_x = pltpu.make_async_copy(
        att.at[:, pl.ds(pl.multiple_of(z * cols, cols), cols)], xz, load_sem.at[0])
    load_x.start()
    load_down = pltpu.make_async_copy(down_hbm, down, load_sem.at[1])
    load_down.start()
    load_up = pltpu.make_async_copy(up_hbm, up, load_sem.at[2])
    load_up.start()
    load_res = pltpu.make_async_copy(res_hbm, res, load_sem.at[3])
    load_res.start()

    barrier = pltpu.get_barrier_semaphore()

    def greet(d, _):
        pl.semaphore_signal(barrier, inc=1, device_id=(lax.rem(me + d, GROUPS), z),
                            device_id_type=MESH)
        return 0

    lax.fori_loop(1, GROUPS, greet, 0)

    def greet_z(d, _):
        pl.semaphore_signal(barrier, inc=1, device_id=(me, lax.rem(z + d, nz)),
                            device_id_type=MESH)
        return 0

    lax.fori_loop(1, nz, greet_z, 0)

    ids = idx_ref[...]
    owner = lax.shift_right_logical(ids, 4)
    local = lax.bitwise_and(ids, CAP - 1)
    hits = (iota((GROUPS, rows), 0) == owner).astype(bf16)
    earlier = (iota((rows, rows), 0) < iota((rows, rows), 1)).astype(bf16)
    before = jnp.dot(hits, earlier, preferred_element_type=f32)
    position = jnp.sum(before * hits.astype(f32), axis=0, keepdims=True)
    target = owner.astype(f32) * CAP + position
    eye = iota((rows, rows), 0) == iota((rows, rows), 1)
    target_col = jnp.sum(jnp.where(eye, target, 0.0), axis=1, keepdims=True)
    local_col = jnp.sum(jnp.where(eye, local.astype(f32), 0.0), axis=1, keepdims=True)
    placing = (iota((slots, rows), 0) == target.astype(i32)).astype(bf16)

    load_x.wait()
    fwd[:, :cols] = jnp.dot(placing, xz[...], preferred_element_type=f32).astype(bf16)
    fwd[:, cols:] = jnp.dot(
        placing, jnp.broadcast_to(local_col, (rows, META)).astype(bf16),
        preferred_element_type=f32).astype(bf16)

    pl.semaphore_wait(barrier, GROUPS - 1 + nz - 1)

    def block(ref, i):
        return ref.at[pl.ds(pl.multiple_of(i * CAP, CAP), CAP), :]

    def send_fwd(d, _):
        to = lax.rem(me + d, GROUPS)
        remote(block(fwd, to), block(got, me), fs.at[to], fr.at[me], to, z).start()
        return 0

    lax.fori_loop(1, GROUPS, send_fwd, 0)
    pltpu.make_async_copy(block(fwd, me), block(got, me), fr.at[me]).start()

    chunk = (par, 3 - par)

    def x_copy(part, dy, dc):
        yd = lax.rem(y + dy, NY)
        cd = lax.rem(core + dc, NC)
        src = att.at[pl.ds(pl.multiple_of(chunk[part] * quarter, quarter), quarter),
                     pl.ds(pl.multiple_of((yd * NC + cd) * kcols, kcols), kcols)]
        dst = xb.at[chunk[part], dc, y]
        if dy == 0 and dc == 0:
            return pltpu.make_async_copy(src, dst, xr.at[part, dc, y])
        return remote(src, dst, xs.at[part, dc, dy], xr.at[part, dc, y], dev(yd, x, cd), z)

    for part in range(2):
        for dy in range(NY):
            for dc in range(NC):
                x_copy(part, dy, dc).start()

    half = lax.div(x, 2)
    spot = lax.rem(x, 2) * NC + core

    def w_copy(dx):
        return remote(w_hbm, wg.at[pl.ds(pl.multiple_of(spot * wblk, wblk), wblk), :],
                      ws.at[dx], wr.at[spot], dev(y, lax.rem(x + dx, NX), half), z)

    for dx in (1, 3, 2):
        w_copy(dx).start()

    @pl.when(half == core)
    def _():
        pltpu.make_async_copy(
            w_hbm, wg.at[pl.ds(pl.multiple_of(spot * wblk, wblk), wblk), :], wr.at[spot]).start()

    @pl.when(half != core)
    def _():
        w_copy(0).start()

    def e_copy(part, rel, yy):
        if part == 0:
            to = z + 1 - 2 * par
        else:
            to = lax.rem(z + nz - 1 + 2 * par, nz)
        ref = xb.at[chunk[part], rel, yy]
        return remote(ref, ref, es.at[part, rel, yy], er.at[part, rel, yy], me, to)

    def x_arrived(part, rel, yy):
        ref = xb.at[chunk[part], rel, yy]
        pltpu.make_async_copy(ref, ref, xr.at[part, rel, yy]).wait()

    def forward(i, _):
        yy = lax.rem(i, NY)
        rel = lax.div(i, NY)
        for part in range(2):
            x_arrived(part, rel, yy)
            e_copy(part, rel, yy).start()
        return 0

    lax.fori_loop(0, NY * NC, forward, 0)

    def got_fwd(s, _):
        pltpu.make_async_copy(block(got, s), block(got, s), fr.at[s]).wait()
        return 0

    lax.fori_loop(0, GROUPS, got_fwd, 0)
    load_down.wait()
    lane = iota((slots, 128), 1)
    mine = got[:, cols:].astype(f32) - (lane >= 64).astype(f32)
    acc = jnp.zeros((slots, 128), f32)
    for t in range(4):
        projected = lax.dot_general(
            got[:, :cols], down[t * 256:(t + 1) * 256, :], (((1,), (1,)), ((), ())),
            preferred_element_type=f32)
        for u in range(2):
            acc += jnp.where(mine == 2.0 * (2 * t + u), projected[:, u * 128:(u + 1) * 128], 0.0)
    acc = acc + pltpu.roll(acc, 64, 1)
    first = iota((slots // 2, 128), 1) < 64
    low_own[...] = jnp.where(first, acc[:slots // 2], acc[slots // 2:]).reshape(low_own.shape)

    def low_send(d, _):
        to = lax.rem(z + d, nz)
        remote(low_own.at[to], low_in.at[z], ls.at[to], lr.at[z], me, to).start()
        return 0

    lax.fori_loop(1, nz, low_send, 0)

    def w_arrived(p, _):
        ref = wg.at[pl.ds(pl.multiple_of(p * wblk, wblk), wblk), :]
        pltpu.make_async_copy(ref, ref, wr.at[p]).wait()
        return 0

    lax.fori_loop(0, 4, w_arrived, 0)

    def base(k):
        place = pl.ds(pl.multiple_of(k * quarter, quarter), quarter)
        tile = min(256, cols)

        def one(n, _):
            at = pl.ds(pl.multiple_of(n * tile, tile), tile)
            r = jnp.dot(xb[k].reshape(NC * NY * quarter, kcols), wg[:, at],
                        preferred_element_type=f32)
            r = r.reshape(NC, NY, quarter, tile)
            keep[:, place, at] = r[0]
            sib_out[:, place, at] = r[1].astype(bf16)
            return 0

        lax.fori_loop(0, cols // tile, one, 0)

    base(chunk[0])
    base(chunk[1])

    def low_got(d, total):
        s = lax.rem(z + d, nz)
        pltpu.make_async_copy(low_in.at[s], low_in.at[s], lr.at[s]).wait()
        return total + low_in[s]

    low_sum[...] = lax.fori_loop(1, nz, low_got, low_own[z]).astype(bf16)

    def low_spread(d, _):
        to = lax.rem(z + d, nz)
        remote(low_sum, low_all.at[z], gs.at[to], gr.at[z], me, to).start()
        return 0

    lax.fori_loop(1, nz, low_spread, 0)
    low_all[z] = low_sum[...]

    other = (1 - par, 2 + par)

    def e_arrived(i, _):
        yy = lax.rem(i, NY)
        rel = lax.div(i, NY)
        for part in range(2):
            ref = xb.at[other[part], rel, yy]
            pltpu.make_async_copy(ref, ref, er.at[part, rel, yy]).wait()
        return 0

    lax.fori_loop(0, NY * NC, e_arrived, 0)
    base(other[0])
    base(other[1])

    def pair_copy(yy):
        return remote(sib_out.at[yy], sib_in.at[yy], ps.at[yy], pr.at[yy],
                      dev(y, x, 1 - core), z)

    for dy in (2, 1, 3, 0):
        pair_copy(lax.rem(y + dy, NY)).start()

    def low_here(d, _):
        s = lax.rem(z + d, nz)
        pltpu.make_async_copy(low_all.at[s], low_all.at[s], gr.at[s]).wait()
        return 0

    lax.fori_loop(1, nz, low_here, 0)
    load_up.wait()
    packed = low_all[...].reshape(slots // 2, 128).astype(f32)
    turned = pltpu.roll(packed, 64, 1)
    low = jnp.concatenate(
        [jnp.where(first, packed, turned), jnp.where(first, turned, packed)], axis=0)
    for j in range(8):
        spread[:, j * 128:(j + 1) * 128] = jnp.where(mine == 2.0 * j, low, 0.0).astype(bf16)
    tile = min(256, cols)

    def up_tile(n, _):
        at = pl.ds(pl.multiple_of(n * tile, tile), tile)
        delta[:, at] = (jnp.dot(spread[...], up[:, at], preferred_element_type=f32)
                        * adapter_scale).astype(bf16)
        return 0

    lax.fori_loop(0, cols // tile, up_tile, 0)

    def send_back(d, _):
        to = lax.rem(me + d, GROUPS)
        remote(block(delta, to), block(back, me), bs.at[to], br.at[me], to, z).start()
        return 0

    lax.fori_loop(1, GROUPS, send_back, 0)
    pltpu.make_async_copy(block(delta, me), block(back, me), br.at[me]).start()

    def sum_copy(dy):
        yd = lax.rem(y + dy, NY)
        return remote(sum_out.at[dy], sum_in.at[dy], rs.at[dy], rr.at[dy], dev(yd, x, core), z)

    for dy in (2, 1, 3, 0):
        yd = lax.rem(y + dy, NY)
        pltpu.make_async_copy(sib_in.at[yd], sib_in.at[yd], pr.at[yd]).wait()
        if dy == 0:
            keep[yd] = keep[yd] + sib_in[yd].astype(f32)
        else:
            sum_out[dy] = (keep[yd] + sib_in[yd].astype(f32)).astype(bf16)
            sum_copy(dy).start()

    load_res.wait()
    for dy in (1, 3, 2):
        pltpu.make_async_copy(sum_in.at[dy], sum_in.at[dy], rr.at[dy]).wait()
    total = (res[...].astype(f32) + keep[y] + sum_in[1].astype(f32) + sum_in[2].astype(f32)
             + sum_in[3].astype(f32))
    homing = (iota((rows, slots), 1) == target_col.astype(i32)).astype(bf16)

    def got_back(s, _):
        pltpu.make_async_copy(block(back, s), block(back, s), br.at[s]).wait()
        return 0

    lax.fori_loop(0, GROUPS, got_back, 0)
    total = total + jnp.dot(homing, back[...], preferred_element_type=f32)
    out_ref[...] = total.astype(bf16)

    def sent(d, _):
        to = lax.rem(me + d, GROUPS)
        remote(block(fwd, to), block(got, me), fs.at[to], fr.at[me], to, z).wait_send()
        remote(block(delta, to), block(back, me), bs.at[to], br.at[me], to, z).wait_send()
        return 0

    lax.fori_loop(1, GROUPS, sent, 0)

    def sent_z(d, _):
        to = lax.rem(z + d, nz)
        remote(low_own.at[to], low_in.at[z], ls.at[to], lr.at[z], me, to).wait_send()
        remote(low_sum, low_all.at[z], gs.at[to], gr.at[z], me, to).wait_send()
        return 0

    lax.fori_loop(1, nz, sent_z, 0)
    for part in range(2):
        for dy in range(NY):
            for dc in range(NC):
                if dy or dc:
                    x_copy(part, dy, dc).wait_send()
                e_copy(part, dc, dy).wait_send()
    for dx in (1, 2, 3):
        w_copy(dx).wait_send()
        sum_copy(dx).wait_send()

    @pl.when(half != core)
    def _():
        w_copy(0).wait_send()

    for dy in range(NY):
        pair_copy(dy).wait_send()


def per_device(
    attended, residual, output_matrix, adapter_down_weight, adapter_up_weight, request_adapter_index
):
    nz = lax.axis_size("tensor")
    rows, width = attended.shape
    cols = width // nz
    kcols = width // (NY * NC)
    adapters, rank, unused_value = adapter_down_weight.shape
    slots = GROUPS * CAP
    wide = adapters * rank
    quarter = rows // 4
    dma = pltpu.SemaphoreType.DMA
    anyspace = pl.BlockSpec(memory_space=pl.ANY)
    vmem = pl.BlockSpec(memory_space=pltpu.VMEM)
    return pl.pallas_call(
        functools.partial(kernel, nz),
        out_shape=jax.ShapeDtypeStruct((rows, cols), bf16),
        in_specs=[vmem] + [anyspace] * 5,
        out_specs=vmem,
        scratch_shapes=[
            pltpu.VMEM((rows, cols), bf16),
            pltpu.VMEM((rows, cols), bf16),
            pltpu.VMEM((wide, cols), bf16),
            pltpu.VMEM((wide, cols), bf16),
            pltpu.VMEM((slots, cols + META), bf16),
            pltpu.VMEM((slots, cols + META), bf16),
            pltpu.VMEM((nz, slots // 2 // nz, 128), f32),
            pltpu.VMEM((nz, slots // 2 // nz, 128), f32),
            pltpu.VMEM((slots // 2 // nz, 128), bf16),
            pltpu.VMEM((nz, slots // 2 // nz, 128), bf16),
            pltpu.VMEM((slots, wide), bf16),
            pltpu.VMEM((slots, cols), bf16),
            pltpu.VMEM((slots, cols), bf16),
            pltpu.VMEM((4, NC, NY, quarter, kcols), bf16),
            pltpu.VMEM((kcols, cols), bf16),
            pltpu.VMEM((NY, rows, cols), f32),
            pltpu.VMEM((NY, rows, cols), bf16),
            pltpu.VMEM((NY, rows, cols), bf16),
            pltpu.VMEM((NY, rows, cols), bf16),
            pltpu.VMEM((NY, rows, cols), bf16),
            dma((4,)),
            dma((GROUPS,)), dma((GROUPS,)),
            dma((GROUPS,)), dma((GROUPS,)),
            dma((nz,)), dma((nz,)),
            dma((nz,)), dma((nz,)),
            dma((2, NC, NY)), dma((2, NC, NY)),
            dma((2, NC, NY)), dma((2, NC, NY)),
            dma((4,)), dma((4,)),
            dma((NY,)), dma((NY,)),
            dma((NY,)), dma((NY,)),
        ],
        compiler_params=pltpu.CompilerParams(
            collective_id=0, has_side_effects=True, vmem_limit_bytes=60 * 1024 * 1024),
    )(
        request_adapter_index.reshape(1, rows), attended, residual, output_matrix,
        adapter_down_weight.reshape(wide, cols), adapter_up_weight.reshape(wide, cols),
    )


def solution(mesh):
    return jax.shard_map(
        per_device,
        mesh=mesh,
        in_specs=(
            P("adapter", None),
            P("adapter", "tensor"),
            P("adapter", "tensor"),
            P("adapter", None, "tensor"),
            P("adapter", None, "tensor"),
            P("adapter"),
        ),
        out_specs=P("adapter", "tensor"),
        check_vma=False,
    )
```

```python
import functools

import jax
import jax.numpy as jnp
from jax import lax
from jax.experimental import pallas as pl
from jax.experimental.pallas import tpu as pltpu
from jax.sharding import PartitionSpec as P

adapter_scale = 2.0
NY, NX, NC = 4, 4, 2
GROUPS = NY * NX * NC
CAP = 16
META = 128
MESH = pl.DeviceIdType.MESH
FAR_FIRST = sorted(
    ((dy, dx, dc) for dy in range(NY) for dx in range(NX) for dc in range(NC) if dy or dx or dc),
    key=lambda o: -min(o[0], NY - o[0]) - min(o[1], NX - o[1]))
f32, bf16, i32 = jnp.float32, jnp.bfloat16, jnp.int32


def iota(shape, dim):
    return lax.broadcasted_iota(i32, shape, dim)


def kernel(
    nz, idx_ref, att, res_hbm, w_hbm, down_hbm, up_hbm, out_ref,
    xz, res, down, up, fwd, got, low_own, low_in, low_sum, low_all, spread, delta, back,
    xb, wg, keep, sib_out, sib_in, sum_out, sum_in,
    load_sem, fs, fr, bs, br, ls, lr, gs, gr, xs, xr, es, er, hs, hr, ws, wr, vs, ps, pr, rs, rr,
):
    me = lax.axis_index("adapter")
    z = lax.axis_index("tensor")
    core = lax.rem(me, NC)
    x = lax.rem(lax.div(me, NC), NX)
    y = lax.div(me, NC * NX)
    mine_q = lax.rem(z, 4)
    rows, cols = out_ref.shape
    slots = GROUPS * CAP
    kcols = xb.shape[-1]
    quarter = rows // 4
    wblk = w_hbm.shape[0]

    def dev(yy, xx, cc):
        return (yy * NX + xx) * NC + cc

    def remote(src, dst, ssem, rsem, a, t):
        return pltpu.make_async_remote_copy(
            src_ref=src, dst_ref=dst, send_sem=ssem, recv_sem=rsem,
            device_id=(a, t), device_id_type=MESH)

    load_x = pltpu.make_async_copy(
        att.at[:, pl.ds(pl.multiple_of(z * cols, cols), cols)], xz, load_sem.at[0])
    load_x.start()
    load_down = pltpu.make_async_copy(down_hbm, down, load_sem.at[1])
    load_down.start()
    load_up = pltpu.make_async_copy(up_hbm, up, load_sem.at[2])
    load_up.start()
    load_res = pltpu.make_async_copy(res_hbm, res, load_sem.at[3])
    load_res.start()

    barrier = pltpu.get_barrier_semaphore()

    def greet(d, _):
        pl.semaphore_signal(barrier, inc=1, device_id=(lax.rem(me + d, GROUPS), z),
                            device_id_type=MESH)
        return 0

    lax.fori_loop(1, GROUPS, greet, 0)

    def greet_z(d, _):
        pl.semaphore_signal(barrier, inc=1, device_id=(me, lax.rem(z + d, nz)),
                            device_id_type=MESH)
        return 0

    lax.fori_loop(1, nz, greet_z, 0)

    ids = idx_ref[...]
    owner = lax.shift_right_logical(ids, 4)
    local = lax.bitwise_and(ids, CAP - 1)
    hits = (iota((GROUPS, rows), 0) == owner).astype(bf16)
    earlier = (iota((rows, rows), 0) < iota((rows, rows), 1)).astype(bf16)
    before = jnp.dot(hits, earlier, preferred_element_type=f32)
    position = jnp.sum(before * hits.astype(f32), axis=0, keepdims=True)
    target = owner.astype(f32) * CAP + position
    eye = iota((rows, rows), 0) == iota((rows, rows), 1)
    target_col = jnp.sum(jnp.where(eye, target, 0.0), axis=1, keepdims=True)
    local_col = jnp.sum(jnp.where(eye, local.astype(f32), 0.0), axis=1, keepdims=True)
    placing = (iota((slots, rows), 0) == target.astype(i32)).astype(bf16)

    load_x.wait()
    fwd[:, :cols] = jnp.dot(placing, xz[...], preferred_element_type=f32).astype(bf16)
    fwd[:, cols:] = jnp.dot(
        placing, jnp.broadcast_to(local_col, (rows, META)).astype(bf16),
        preferred_element_type=f32).astype(bf16)

    pl.semaphore_wait(barrier, GROUPS - 1 + nz - 1)

    def block(ref, i):
        return ref.at[pl.ds(pl.multiple_of(i * CAP, CAP), CAP), :]

    def fwd_copy(to):
        return remote(block(fwd, to), block(got, me), fs.at[to], fr.at[me], to, z)

    def x_copy(dy, dc):
        yd = lax.rem(y + dy, NY)
        cd = lax.rem(core + dc, NC)
        src = att.at[pl.ds(pl.multiple_of(mine_q * quarter, quarter), quarter),
                     pl.ds(pl.multiple_of((yd * NC + cd) * kcols, kcols), kcols)]
        dst = xb.at[mine_q, dc, y]
        if dy == 0 and dc == 0:
            return pltpu.make_async_copy(src, dst, xr.at[dc, y])
        return remote(src, dst, xs.at[dc, dy], xr.at[dc, y], dev(yd, x, cd), z)

    def send_x():
        for dy in (2, 1, 3, 0):
            for dc in range(NC):
                x_copy(dy, dc).start()

    send_x()
    for dy, dx, dc in FAR_FIRST:
        fwd_copy(dev(lax.rem(y + dy, NY), lax.rem(x + dx, NX), lax.rem(core + dc, NC))).start()
    pltpu.make_async_copy(block(fwd, me), block(got, me), fr.at[me]).start()

    half = lax.div(x, 2)
    spot = lax.rem(x, 2) * NC + core
    hblk = wblk // 2

    def w_part(p, h):
        return wg.at[pl.ds(pl.multiple_of(p * wblk + h * hblk, hblk), hblk), :]

    def w_copy(dx, h):
        return remote(w_hbm.at[pl.ds(h * hblk, hblk), :], w_part(spot, h), ws.at[dx, h],
                      wr.at[spot, h], dev(y, lax.rem(x + dx, NX), half), z)

    def send_w():
        for i in range(2):
            w_copy(1, i).start()
            w_copy(3, 1 - i).start()

        @pl.when(half == core)
        def _():
            for h in range(2):
                pltpu.make_async_copy(w_hbm.at[pl.ds(h * hblk, hblk), :], w_part(spot, h),
                                      wr.at[spot, h]).start()

        @pl.when(half != core)
        def _():
            for h in range(2):
                w_copy(0, h).start()

    ahead = lax.rem(x - 2 * core + NX, NX)
    near = lax.rem(ahead + 1, 2)
    side = 1 - lax.rem(lax.div(ahead + 1, 2), 2)

    def w_pass(c):
        part = w_part(near * NC + c, side)
        return remote(part, part, vs.at[c], wr.at[near * NC + c, side],
                      dev(y, lax.rem(x + 1 + 2 * side, NX), core), z)

    def w_arrived(p, h):
        pltpu.make_async_copy(w_part(p, h), w_part(p, h), wr.at[p, h]).wait()

    right, left = lax.rem(z + 1, nz), lax.rem(z + nz - 1, nz)
    left_q, right_q, far_q = lax.rem(mine_q + 3, 4), lax.rem(mine_q + 1, 4), lax.rem(mine_q + 2, 4)

    def e_copy(way, rel, yy):
        ref = xb.at[mine_q, rel, yy]
        return remote(ref, ref, es.at[way, rel, yy], er.at[way, rel, yy], me, (right, left)[way])

    def h_copy(way, yy):
        ref = xb.at[(left_q, right_q)[way], way, yy]
        return remote(ref, ref, hs.at[way, yy], hr.at[way, yy], me, (right, left)[way])

    def arrived(q, rel, yy, sem):
        ref = xb.at[q, rel, yy]
        pltpu.make_async_copy(ref, ref, sem).wait()

    def share(i, _):
        yy = lax.rem(i, NY)
        rel = lax.div(i, NY)
        arrived(mine_q, rel, yy, xr.at[rel, yy])
        e_copy(0, rel, yy).start()
        e_copy(1, rel, yy).start()
        return 0

    def share_on(yy, _):
        for way in range(2):
            arrived((left_q, right_q)[way], way, yy, er.at[way, way, yy])
            h_copy(way, yy).start()
        return 0

    lax.fori_loop(0, NY * NC, share, 0)
    send_w()

    def got_fwd(s, _):
        pltpu.make_async_copy(block(got, s), block(got, s), fr.at[s]).wait()
        return 0

    lax.fori_loop(0, GROUPS, got_fwd, 0)
    load_down.wait()
    lane = iota((slots, 128), 1)
    mine = got[:, cols:].astype(f32) - (lane >= 64).astype(f32)
    acc = jnp.zeros((slots, 128), f32)
    for t in range(4):
        projected = lax.dot_general(
            got[:, :cols], down[t * 256:(t + 1) * 256, :], (((1,), (1,)), ((), ())),
            preferred_element_type=f32)
        for u in range(2):
            acc += jnp.where(mine == 2.0 * (2 * t + u), projected[:, u * 128:(u + 1) * 128], 0.0)
    acc = acc + pltpu.roll(acc, 64, 1)
    first = iota((slots // 2, 128), 1) < 64
    low_own[...] = jnp.where(first, acc[:slots // 2], acc[slots // 2:]).reshape(low_own.shape)

    def low_send(d, _):
        to = lax.rem(z + d, nz)
        remote(low_own.at[to], low_in.at[z], ls.at[to], lr.at[z], me, to).start()
        return 0

    lax.fori_loop(1, nz, low_send, 0)

    def base(k):
        place = pl.ds(pl.multiple_of(k * quarter, quarter), quarter)
        tile = min(256, cols)

        def one(n, _):
            at = pl.ds(pl.multiple_of(n * tile, tile), tile)
            r = jnp.dot(xb[k].reshape(NC * NY * quarter, kcols), wg[:, at],
                        preferred_element_type=f32)
            r = r.reshape(NC, NY, quarter, tile)
            keep[:, place, at] = r[0]
            sib_out[:, place, at] = r[1].astype(bf16)
            return 0

        lax.fori_loop(0, cols // tile, one, 0)

    for c in range(NC):
        w_arrived(near * NC + c, side)
        w_pass(c).start()

    def low_got(d, total):
        s = lax.rem(z + d, nz)
        pltpu.make_async_copy(low_in.at[s], low_in.at[s], lr.at[s]).wait()
        return total + low_in[s]

    low_sum[...] = lax.fori_loop(1, nz, low_got, low_own[z]).astype(bf16)

    def low_spread(d, _):
        to = lax.rem(z + d, nz)
        remote(low_sum, low_all.at[z], gs.at[to], gr.at[z], me, to).start()
        return 0

    lax.fori_loop(1, nz, low_spread, 0)
    low_all[z] = low_sum[...]

    def up_and_back():
        def low_here(d, _):
            s = lax.rem(z + d, nz)
            pltpu.make_async_copy(low_all.at[s], low_all.at[s], gr.at[s]).wait()
            return 0

        lax.fori_loop(1, nz, low_here, 0)
        load_up.wait()
        packed = low_all[...].reshape(slots // 2, 128).astype(f32)
        turned = pltpu.roll(packed, 64, 1)
        low = jnp.concatenate(
            [jnp.where(first, packed, turned), jnp.where(first, turned, packed)], axis=0)
        for j in range(8):
            spread[:, j * 128:(j + 1) * 128] = jnp.where(mine == 2.0 * j, low, 0.0).astype(bf16)
        tile = min(256, cols)

        def up_tile(n, _):
            at = pl.ds(pl.multiple_of(n * tile, tile), tile)
            delta[:, at] = (jnp.dot(spread[...], up[:, at], preferred_element_type=f32)
                            * adapter_scale).astype(bf16)
            return 0

        lax.fori_loop(0, cols // tile, up_tile, 0)

        for dy, dx, dc in FAR_FIRST:
            to = dev(lax.rem(y + dy, NY), lax.rem(x + dx, NX), lax.rem(core + dc, NC))
            remote(block(delta, to), block(back, me), bs.at[to], br.at[me], to, z).start()
        pltpu.make_async_copy(block(delta, me), block(back, me), br.at[me]).start()

    up_and_back()
    lax.fori_loop(0, NY, share_on, 0)

    for c in range(NC):
        w_arrived(near * NC + c, 1 - side)
        w_arrived((1 - near) * NC + c, 0)
        w_arrived((1 - near) * NC + c, 1)
    base(mine_q)

    def from_sides(yy, _):
        arrived(left_q, 1, yy, er.at[0, 1, yy])
        arrived(right_q, 0, yy, er.at[1, 0, yy])
        return 0

    lax.fori_loop(0, NY, from_sides, 0)
    base(left_q)
    base(right_q)

    def from_far(yy, _):
        for way in range(2):
            arrived(far_q, way, yy, hr.at[way, yy])
        return 0

    lax.fori_loop(0, NY, from_far, 0)
    base(far_q)

    def pair_copy(yy):
        return remote(sib_out.at[yy], sib_in.at[yy], ps.at[yy], pr.at[yy],
                      dev(y, x, 1 - core), z)

    for dy in (2, 1, 3, 0):
        pair_copy(lax.rem(y + dy, NY)).start()

    def sum_copy(dy):
        yd = lax.rem(y + dy, NY)
        return remote(sum_out.at[dy], sum_in.at[dy], rs.at[dy], rr.at[dy], dev(yd, x, core), z)

    for dy in (2, 1, 3, 0):
        yd = lax.rem(y + dy, NY)
        pltpu.make_async_copy(sib_in.at[yd], sib_in.at[yd], pr.at[yd]).wait()
        if dy == 0:
            keep[yd] = keep[yd] + sib_in[yd].astype(f32)
        else:
            sum_out[dy] = (keep[yd] + sib_in[yd].astype(f32)).astype(bf16)
            sum_copy(dy).start()

    load_res.wait()
    for dy in (1, 3, 2):
        pltpu.make_async_copy(sum_in.at[dy], sum_in.at[dy], rr.at[dy]).wait()
    total = (res[...].astype(f32) + keep[y] + sum_in[1].astype(f32) + sum_in[2].astype(f32)
             + sum_in[3].astype(f32))
    homing = (iota((rows, slots), 1) == target_col.astype(i32)).astype(bf16)

    def got_back(s, _):
        pltpu.make_async_copy(block(back, s), block(back, s), br.at[s]).wait()
        return 0

    lax.fori_loop(0, GROUPS, got_back, 0)
    total = total + jnp.dot(homing, back[...], preferred_element_type=f32)
    out_ref[...] = total.astype(bf16)

    def sent(d, _):
        to = lax.rem(me + d, GROUPS)
        remote(block(fwd, to), block(got, me), fs.at[to], fr.at[me], to, z).wait_send()
        remote(block(delta, to), block(back, me), bs.at[to], br.at[me], to, z).wait_send()
        return 0

    lax.fori_loop(1, GROUPS, sent, 0)

    def sent_z(d, _):
        to = lax.rem(z + d, nz)
        remote(low_own.at[to], low_in.at[z], ls.at[to], lr.at[z], me, to).wait_send()
        remote(low_sum, low_all.at[z], gs.at[to], gr.at[z], me, to).wait_send()
        return 0

    lax.fori_loop(1, nz, sent_z, 0)
    for dy in range(NY):
        for dc in range(NC):
            if dy or dc:
                x_copy(dy, dc).wait_send()
            for way in range(2):
                e_copy(way, dc, dy).wait_send()
        for way in range(2):
            h_copy(way, dy).wait_send()
    for dx in (1, 3):
        for h in range(2):
            w_copy(dx, h).wait_send()
    for dx in (1, 2, 3):
        sum_copy(dx).wait_send()
    for c in range(NC):
        w_pass(c).wait_send()

    @pl.when(half != core)
    def _():
        for h in range(2):
            w_copy(0, h).wait_send()

    for dy in range(NY):
        pair_copy(dy).wait_send()


def per_device(
    attended, residual, output_matrix, adapter_down_weight, adapter_up_weight, request_adapter_index
):
    nz = lax.axis_size("tensor")
    rows, width = attended.shape
    cols = width // nz
    kcols = width // (NY * NC)
    adapters, rank, unused_value = adapter_down_weight.shape
    slots = GROUPS * CAP
    wide = adapters * rank
    quarter = rows // 4
    dma = pltpu.SemaphoreType.DMA
    anyspace = pl.BlockSpec(memory_space=pl.ANY)
    vmem = pl.BlockSpec(memory_space=pltpu.VMEM)
    return pl.pallas_call(
        functools.partial(kernel, nz),
        out_shape=jax.ShapeDtypeStruct((rows, cols), bf16),
        in_specs=[vmem] + [anyspace] * 5,
        out_specs=vmem,
        scratch_shapes=[
            pltpu.VMEM((rows, cols), bf16),
            pltpu.VMEM((rows, cols), bf16),
            pltpu.VMEM((wide, cols), bf16),
            pltpu.VMEM((wide, cols), bf16),
            pltpu.VMEM((slots, cols + META), bf16),
            pltpu.VMEM((slots, cols + META), bf16),
            pltpu.VMEM((nz, slots // 2 // nz, 128), f32),
            pltpu.VMEM((nz, slots // 2 // nz, 128), f32),
            pltpu.VMEM((slots // 2 // nz, 128), bf16),
            pltpu.VMEM((nz, slots // 2 // nz, 128), bf16),
            pltpu.VMEM((slots, wide), bf16),
            pltpu.VMEM((slots, cols), bf16),
            pltpu.VMEM((slots, cols), bf16),
            pltpu.VMEM((4, NC, NY, quarter, kcols), bf16),
            pltpu.VMEM((kcols, cols), bf16),
            pltpu.VMEM((NY, rows, cols), f32),
            pltpu.VMEM((NY, rows, cols), bf16),
            pltpu.VMEM((NY, rows, cols), bf16),
            pltpu.VMEM((NY, rows, cols), bf16),
            pltpu.VMEM((NY, rows, cols), bf16),
            dma((4,)),
            dma((GROUPS,)), dma((GROUPS,)),
            dma((GROUPS,)), dma((GROUPS,)),
            dma((nz,)), dma((nz,)),
            dma((nz,)), dma((nz,)),
            dma((NC, NY)), dma((NC, NY)),
            dma((2, NC, NY)), dma((2, NC, NY)),
            dma((2, NY)), dma((2, NY)),
            dma((4, 2)), dma((4, 2)), dma((NC,)),
            dma((NY,)), dma((NY,)),
            dma((NY,)), dma((NY,)),
        ],
        compiler_params=pltpu.CompilerParams(
            collective_id=0, has_side_effects=True, vmem_limit_bytes=60 * 1024 * 1024),
    )(
        request_adapter_index.reshape(1, rows), attended, residual, output_matrix,
        adapter_down_weight.reshape(wide, cols), adapter_up_weight.reshape(wide, cols),
    )


def solution(mesh):
    return jax.shard_map(
        per_device,
        mesh=mesh,
        in_specs=(
            P("adapter", None),
            P("adapter", "tensor"),
            P("adapter", "tensor"),
            P("adapter", None, "tensor"),
            P("adapter", None, "tensor"),
            P("adapter"),
        ),
        out_specs=P("adapter", "tensor"),
        check_vma=False,
    )
```

```python
import functools

import jax
import jax.numpy as jnp
from jax import lax
from jax.experimental import pallas as pl
from jax.experimental.pallas import tpu as pltpu
from jax.sharding import PartitionSpec as P

adapter_scale = 2.0
NY, NX, NC = 4, 4, 2
GROUPS = NY * NX * NC
CAP = 16
META = 128
MESH = pl.DeviceIdType.MESH
FAR_FIRST = sorted(
    ((dy, dx, dc) for dy in range(NY) for dx in range(NX) for dc in range(NC) if dy or dx or dc),
    key=lambda o: -min(o[0], NY - o[0]) - min(o[1], NX - o[1]))
f32, bf16, i32 = jnp.float32, jnp.bfloat16, jnp.int32


def iota(shape, dim):
    return lax.broadcasted_iota(i32, shape, dim)


def kernel(
    nz, idx_ref, att, res_hbm, w_hbm, down_hbm, up_hbm, out_ref,
    xz, res, down, up, fwd, got, low_own, low_in, low_sum, low_all, spread, delta, back,
    xb, wg, keep, sib_out, sib_in, sum_out, sum_in,
    load_sem, fs, fr, bs, br, ls, lr, gs, gr, xs, xr, es, er, hs, hr, ws, wr, vs, ps, pr, rs, rr,
):
    me = lax.axis_index("adapter")
    z = lax.axis_index("tensor")
    core = lax.rem(me, NC)
    x = lax.rem(lax.div(me, NC), NX)
    y = lax.div(me, NC * NX)
    mine_q = lax.rem(z, 4)
    rows, cols = out_ref.shape
    slots = GROUPS * CAP
    kcols = xb.shape[-1]
    quarter = rows // 4
    wblk = w_hbm.shape[0]
    hcols = cols // 2

    def part_of(g):
        return pl.ds(g * hcols, hcols)

    def dev(yy, xx, cc):
        return (yy * NX + xx) * NC + cc

    def remote(src, dst, ssem, rsem, a, t):
        return pltpu.make_async_remote_copy(
            src_ref=src, dst_ref=dst, send_sem=ssem, recv_sem=rsem,
            device_id=(a, t), device_id_type=MESH)

    load_x = pltpu.make_async_copy(
        att.at[:, pl.ds(pl.multiple_of(z * cols, cols), cols)], xz, load_sem.at[0])
    load_x.start()
    load_down = pltpu.make_async_copy(down_hbm, down, load_sem.at[1])
    load_down.start()
    load_up = pltpu.make_async_copy(up_hbm, up, load_sem.at[2])
    load_up.start()
    load_res = pltpu.make_async_copy(res_hbm, res, load_sem.at[3])
    load_res.start()

    barrier = pltpu.get_barrier_semaphore()

    def greet(d, _):
        pl.semaphore_signal(barrier, inc=1, device_id=(lax.rem(me + d, GROUPS), z),
                            device_id_type=MESH)
        return 0

    lax.fori_loop(1, GROUPS, greet, 0)

    def greet_z(d, _):
        pl.semaphore_signal(barrier, inc=1, device_id=(me, lax.rem(z + d, nz)),
                            device_id_type=MESH)
        return 0

    lax.fori_loop(1, nz, greet_z, 0)

    pl.semaphore_wait(barrier, GROUPS - 1 + nz - 1)

    def block(ref, i):
        return ref.at[pl.ds(pl.multiple_of(i * CAP, CAP), CAP), :]

    def fwd_copy(to):
        return remote(block(fwd, to), block(got, me), fs.at[to], fr.at[me], to, z)

    def x_copy(dy, dc):
        yd = lax.rem(y + dy, NY)
        cd = lax.rem(core + dc, NC)
        src = att.at[pl.ds(pl.multiple_of(mine_q * quarter, quarter), quarter),
                     pl.ds(pl.multiple_of((yd * NC + cd) * kcols, kcols), kcols)]
        dst = xb.at[mine_q, dc, y]
        if dy == 0 and dc == 0:
            return pltpu.make_async_copy(src, dst, xr.at[dc, y])
        return remote(src, dst, xs.at[dc, dy], xr.at[dc, y], dev(yd, x, cd), z)

    def send_x():
        for dy in (2, 1, 3, 0):
            for dc in range(NC):
                x_copy(dy, dc).start()

    send_x()
    half = lax.div(x, 2)
    spot = lax.rem(x, 2) * NC + core
    hblk = wblk // 2

    def w_part(p, h, g):
        return wg.at[pl.ds(pl.multiple_of(p * wblk + h * hblk, hblk), hblk), part_of(g)]

    def w_copy(dx, h, g):
        return remote(w_hbm.at[pl.ds(h * hblk, hblk), part_of(g)], w_part(spot, h, g),
                      ws.at[dx, h, g], wr.at[spot, h, g], dev(y, lax.rem(x + dx, NX), half), z)

    def send_w(g):
        for i in range(2):
            w_copy(1, i, g).start()
            w_copy(3, 1 - i, g).start()

        @pl.when(half == core)
        def _():
            for h in range(2):
                pltpu.make_async_copy(w_hbm.at[pl.ds(h * hblk, hblk), part_of(g)],
                                      w_part(spot, h, g), wr.at[spot, h, g]).start()

        @pl.when(half != core)
        def _():
            for h in range(2):
                w_copy(0, h, g).start()

    ahead = lax.rem(x - 2 * core + NX, NX)
    near = lax.rem(ahead + 1, 2)
    side = 1 - lax.rem(lax.div(ahead + 1, 2), 2)

    def w_pass(c, g):
        part = w_part(near * NC + c, side, g)
        return remote(part, part, vs.at[c, g], wr.at[near * NC + c, side, g],
                      dev(y, lax.rem(x + 1 + 2 * side, NX), core), z)

    def w_arrived(p, h, g):
        part = w_part(p, h, g)
        pltpu.make_async_copy(part, part, wr.at[p, h, g]).wait()

    def pass_on(g):
        for c in range(NC):
            w_arrived(near * NC + c, side, g)
            w_pass(c, g).start()

    def w_ready(g):
        for c in range(NC):
            w_arrived(near * NC + c, 1 - side, g)
            w_arrived((1 - near) * NC + c, 0, g)
            w_arrived((1 - near) * NC + c, 1, g)

    right, left = lax.rem(z + 1, nz), lax.rem(z + nz - 1, nz)
    left_q, right_q, far_q = lax.rem(mine_q + 3, 4), lax.rem(mine_q + 1, 4), lax.rem(mine_q + 2, 4)

    def e_copy(way, rel, yy):
        ref = xb.at[mine_q, rel, yy]
        return remote(ref, ref, es.at[way, rel, yy], er.at[way, rel, yy], me, (right, left)[way])

    def h_copy(way, yy):
        ref = xb.at[(left_q, right_q)[way], way, yy]
        return remote(ref, ref, hs.at[way, yy], hr.at[way, yy], me, (right, left)[way])

    def arrived(q, rel, yy, sem):
        ref = xb.at[q, rel, yy]
        pltpu.make_async_copy(ref, ref, sem).wait()

    def share(i, _):
        yy = lax.rem(i, NY)
        rel = lax.div(i, NY)
        arrived(mine_q, rel, yy, xr.at[rel, yy])
        e_copy(0, rel, yy).start()
        e_copy(1, rel, yy).start()
        return 0

    def share_on(yy, _):
        for way in range(2):
            arrived((left_q, right_q)[way], way, yy, er.at[way, way, yy])
            h_copy(way, yy).start()
        return 0

    send_w(0)
    ids = idx_ref[...]
    owner = lax.shift_right_logical(ids, 4)
    local = lax.bitwise_and(ids, CAP - 1)
    hits = (iota((GROUPS, rows), 0) == owner).astype(bf16)
    earlier = (iota((rows, rows), 0) < iota((rows, rows), 1)).astype(bf16)
    before = jnp.dot(hits, earlier, preferred_element_type=f32)
    position = jnp.sum(before * hits.astype(f32), axis=0, keepdims=True)
    target = owner.astype(f32) * CAP + position
    eye = iota((rows, rows), 0) == iota((rows, rows), 1)
    target_col = jnp.sum(jnp.where(eye, target, 0.0), axis=1, keepdims=True)
    local_col = jnp.sum(jnp.where(eye, local.astype(f32), 0.0), axis=1, keepdims=True)
    placing = (iota((slots, rows), 0) == target.astype(i32)).astype(bf16)

    load_x.wait()
    fwd[:, :cols] = jnp.dot(placing, xz[...], preferred_element_type=f32).astype(bf16)
    fwd[:, cols:] = jnp.dot(
        placing, jnp.broadcast_to(local_col, (rows, META)).astype(bf16),
        preferred_element_type=f32).astype(bf16)

    for dy, dx, dc in FAR_FIRST:
        fwd_copy(dev(lax.rem(y + dy, NY), lax.rem(x + dx, NX), lax.rem(core + dc, NC))).start()
    pltpu.make_async_copy(block(fwd, me), block(got, me), fr.at[me]).start()

    lax.fori_loop(0, NY * NC, share, 0)
    def base(k, g):
        place = pl.ds(pl.multiple_of(k * quarter, quarter), quarter)
        tile = min(256, hcols)

        def one(n, _):
            at = pl.ds(pl.multiple_of(g * hcols + n * tile, tile), tile)
            r = jnp.dot(xb[k].reshape(NC * NY * quarter, kcols), wg[:, at],
                        preferred_element_type=f32)
            r = r.reshape(NC, NY, quarter, tile)
            keep[:, place, at] = r[0]
            sib_out[:, place, at] = r[1].astype(bf16)
            return 0

        lax.fori_loop(0, hcols // tile, one, 0)

    def from_sides(yy, _):
        arrived(left_q, 1, yy, er.at[0, 1, yy])
        arrived(right_q, 0, yy, er.at[1, 0, yy])
        return 0

    def from_far(yy, _):
        for way in range(2):
            arrived(far_q, way, yy, hr.at[way, yy])
        return 0

    def pair_copy(yy, g):
        return remote(sib_out.at[yy, :, part_of(g)], sib_in.at[yy, :, part_of(g)], ps.at[yy, g],
                      pr.at[yy, g], dev(y, x, 1 - core), z)

    def sum_copy(dy, g):
        yd = lax.rem(y + dy, NY)
        return remote(sum_out.at[dy, :, part_of(g)], sum_in.at[dy, :, part_of(g)], rs.at[dy, g],
                      rr.at[dy, g], dev(yd, x, core), z)

    def project_base(g):
        w_ready(g)
        base(mine_q, g)
        if g == 0:
            lax.fori_loop(0, NY, from_sides, 0)
        base(left_q, g)
        base(right_q, g)
        if g == 0:
            lax.fori_loop(0, NY, from_far, 0)
        base(far_q, g)
        for dy in (2, 1, 3, 0):
            pair_copy(lax.rem(y + dy, NY), g).start()

    def send_sum(g):
        at = slice(g * hcols, (g + 1) * hcols)
        for dy in (2, 1, 3, 0):
            yd = lax.rem(y + dy, NY)
            ref = sib_in.at[yd, :, part_of(g)]
            pltpu.make_async_copy(ref, ref, pr.at[yd, g]).wait()
            if dy == 0:
                keep[yd, :, at] = keep[yd, :, at] + sib_in[yd, :, at].astype(f32)
            else:
                sum_out[dy, :, at] = (keep[yd, :, at] + sib_in[yd, :, at].astype(f32)).astype(bf16)
                sum_copy(dy, g).start()

    pass_on(0)
    lax.fori_loop(0, NY, share_on, 0)

    def got_fwd(s, _):
        pltpu.make_async_copy(block(got, s), block(got, s), fr.at[s]).wait()
        return 0

    lax.fori_loop(0, GROUPS, got_fwd, 0)
    send_w(1)
    load_down.wait()
    lane = iota((slots, 128), 1)
    mine = got[:, cols:].astype(f32) - (lane >= 64).astype(f32)
    acc = jnp.zeros((slots, 128), f32)
    for t in range(4):
        projected = lax.dot_general(
            got[:, :cols], down[t * 256:(t + 1) * 256, :], (((1,), (1,)), ((), ())),
            preferred_element_type=f32)
        for u in range(2):
            acc += jnp.where(mine == 2.0 * (2 * t + u), projected[:, u * 128:(u + 1) * 128], 0.0)
    acc = acc + pltpu.roll(acc, 64, 1)
    first = iota((slots // 2, 128), 1) < 64
    low_own[...] = jnp.where(first, acc[:slots // 2], acc[slots // 2:]).reshape(low_own.shape)

    def low_send(d, _):
        to = lax.rem(z + d, nz)
        remote(low_own.at[to], low_in.at[z], ls.at[to], lr.at[z], me, to).start()
        return 0

    lax.fori_loop(1, nz, low_send, 0)

    def low_got(d, total):
        s = lax.rem(z + d, nz)
        pltpu.make_async_copy(low_in.at[s], low_in.at[s], lr.at[s]).wait()
        return total + low_in[s]

    low_sum[...] = lax.fori_loop(1, nz, low_got, low_own[z]).astype(bf16)

    def low_spread(d, _):
        to = lax.rem(z + d, nz)
        remote(low_sum, low_all.at[z], gs.at[to], gr.at[z], me, to).start()
        return 0

    lax.fori_loop(1, nz, low_spread, 0)
    low_all[z] = low_sum[...]

    def up_and_back():
        def low_here(d, _):
            s = lax.rem(z + d, nz)
            pltpu.make_async_copy(low_all.at[s], low_all.at[s], gr.at[s]).wait()
            return 0

        lax.fori_loop(1, nz, low_here, 0)
        load_up.wait()
        packed = low_all[...].reshape(slots // 2, 128).astype(f32)
        turned = pltpu.roll(packed, 64, 1)
        low = jnp.concatenate(
            [jnp.where(first, packed, turned), jnp.where(first, turned, packed)], axis=0)
        for j in range(8):
            spread[:, j * 128:(j + 1) * 128] = jnp.where(mine == 2.0 * j, low, 0.0).astype(bf16)
        tile = min(256, cols)

        def up_tile(n, _):
            at = pl.ds(pl.multiple_of(n * tile, tile), tile)
            delta[:, at] = (jnp.dot(spread[...], up[:, at], preferred_element_type=f32)
                            * adapter_scale).astype(bf16)
            return 0

        lax.fori_loop(0, cols // tile, up_tile, 0)

        for dy, dx, dc in FAR_FIRST:
            to = dev(lax.rem(y + dy, NY), lax.rem(x + dx, NX), lax.rem(core + dc, NC))
            remote(block(delta, to), block(back, me), bs.at[to], br.at[me], to, z).start()
        pltpu.make_async_copy(block(delta, me), block(back, me), br.at[me]).start()

    project_base(0)
    pass_on(1)
    send_sum(0)
    up_and_back()
    project_base(1)
    send_sum(1)

    load_res.wait()
    for g in range(2):
        for dy in (1, 3, 2):
            ref = sum_in.at[dy, :, part_of(g)]
            pltpu.make_async_copy(ref, ref, rr.at[dy, g]).wait()
    total = (res[...].astype(f32) + keep[y] + sum_in[1].astype(f32) + sum_in[2].astype(f32)
             + sum_in[3].astype(f32))
    homing = (iota((rows, slots), 1) == target_col.astype(i32)).astype(bf16)

    def got_back(s, _):
        pltpu.make_async_copy(block(back, s), block(back, s), br.at[s]).wait()
        return 0

    lax.fori_loop(0, GROUPS, got_back, 0)
    total = total + jnp.dot(homing, back[...], preferred_element_type=f32)
    out_ref[...] = total.astype(bf16)

    def sent(d, _):
        to = lax.rem(me + d, GROUPS)
        remote(block(fwd, to), block(got, me), fs.at[to], fr.at[me], to, z).wait_send()
        remote(block(delta, to), block(back, me), bs.at[to], br.at[me], to, z).wait_send()
        return 0

    lax.fori_loop(1, GROUPS, sent, 0)

    def sent_z(d, _):
        to = lax.rem(z + d, nz)
        remote(low_own.at[to], low_in.at[z], ls.at[to], lr.at[z], me, to).wait_send()
        remote(low_sum, low_all.at[z], gs.at[to], gr.at[z], me, to).wait_send()
        return 0

    lax.fori_loop(1, nz, sent_z, 0)
    for dy in range(NY):
        for dc in range(NC):
            if dy or dc:
                x_copy(dy, dc).wait_send()
            for way in range(2):
                e_copy(way, dc, dy).wait_send()
        for way in range(2):
            h_copy(way, dy).wait_send()
    for g in range(2):
        for dx in (1, 3):
            for h in range(2):
                w_copy(dx, h, g).wait_send()
        for dx in (1, 2, 3):
            sum_copy(dx, g).wait_send()
        for c in range(NC):
            w_pass(c, g).wait_send()
        for dy in range(NY):
            pair_copy(dy, g).wait_send()

    @pl.when(half != core)
    def _():
        for g in range(2):
            for h in range(2):
                w_copy(0, h, g).wait_send()


def per_device(
    attended, residual, output_matrix, adapter_down_weight, adapter_up_weight, request_adapter_index
):
    nz = lax.axis_size("tensor")
    rows, width = attended.shape
    cols = width // nz
    kcols = width // (NY * NC)
    adapters, rank, unused_value = adapter_down_weight.shape
    slots = GROUPS * CAP
    wide = adapters * rank
    quarter = rows // 4
    dma = pltpu.SemaphoreType.DMA
    anyspace = pl.BlockSpec(memory_space=pl.ANY)
    vmem = pl.BlockSpec(memory_space=pltpu.VMEM)
    return pl.pallas_call(
        functools.partial(kernel, nz),
        out_shape=jax.ShapeDtypeStruct((rows, cols), bf16),
        in_specs=[vmem] + [anyspace] * 5,
        out_specs=vmem,
        scratch_shapes=[
            pltpu.VMEM((rows, cols), bf16),
            pltpu.VMEM((rows, cols), bf16),
            pltpu.VMEM((wide, cols), bf16),
            pltpu.VMEM((wide, cols), bf16),
            pltpu.VMEM((slots, cols + META), bf16),
            pltpu.VMEM((slots, cols + META), bf16),
            pltpu.VMEM((nz, slots // 2 // nz, 128), f32),
            pltpu.VMEM((nz, slots // 2 // nz, 128), f32),
            pltpu.VMEM((slots // 2 // nz, 128), bf16),
            pltpu.VMEM((nz, slots // 2 // nz, 128), bf16),
            pltpu.VMEM((slots, wide), bf16),
            pltpu.VMEM((slots, cols), bf16),
            pltpu.VMEM((slots, cols), bf16),
            pltpu.VMEM((4, NC, NY, quarter, kcols), bf16),
            pltpu.VMEM((kcols, cols), bf16),
            pltpu.VMEM((NY, rows, cols), f32),
            pltpu.VMEM((NY, rows, cols), bf16),
            pltpu.VMEM((NY, rows, cols), bf16),
            pltpu.VMEM((NY, rows, cols), bf16),
            pltpu.VMEM((NY, rows, cols), bf16),
            dma((4,)),
            dma((GROUPS,)), dma((GROUPS,)),
            dma((GROUPS,)), dma((GROUPS,)),
            dma((nz,)), dma((nz,)),
            dma((nz,)), dma((nz,)),
            dma((NC, NY)), dma((NC, NY)),
            dma((2, NC, NY)), dma((2, NC, NY)),
            dma((2, NY)), dma((2, NY)),
            dma((4, 2, 2)), dma((4, 2, 2)), dma((NC, 2)),
            dma((NY, 2)), dma((NY, 2)),
            dma((NY, 2)), dma((NY, 2)),
        ],
        compiler_params=pltpu.CompilerParams(
            collective_id=0, has_side_effects=True, vmem_limit_bytes=60 * 1024 * 1024),
    )(
        request_adapter_index.reshape(1, rows), attended, residual, output_matrix,
        adapter_down_weight.reshape(wide, cols), adapter_up_weight.reshape(wide, cols),
    )


def solution(mesh):
    return jax.shard_map(
        per_device,
        mesh=mesh,
        in_specs=(
            P("adapter", None),
            P("adapter", "tensor"),
            P("adapter", "tensor"),
            P("adapter", None, "tensor"),
            P("adapter", None, "tensor"),
            P("adapter"),
        ),
        out_specs=P("adapter", "tensor"),
        check_vma=False,
    )
```

```python
import functools

import jax
import jax.numpy as jnp
from jax import lax
from jax.experimental import pallas as pl
from jax.experimental.pallas import tpu as pltpu
from jax.sharding import PartitionSpec as P

adapter_scale = 2.0
NY, NX, NC = 4, 4, 2
GROUPS = NY * NX * NC
CAP = 16
META = 128
MESH = pl.DeviceIdType.MESH
FAR_FIRST = sorted(
    ((dy, dx, dc) for dy in range(NY) for dx in range(NX) for dc in range(NC) if dy or dx or dc),
    key=lambda o: (-min(o[0], NY - o[0]) - min(o[1], NX - o[1]), o[2]))
f32, bf16, i32 = jnp.float32, jnp.bfloat16, jnp.int32


def iota(shape, dim):
    return lax.broadcasted_iota(i32, shape, dim)


def kernel(
    nz, idx_ref, att, res_hbm, w_hbm, down_hbm, up_hbm, out_ref,
    xz, res, down, up, fwd, got, low_own, low_in, low_sum, low_all, spread, delta, back,
    xb, wg, keep, sib_out, sib_in, sum_out, sum_in,
    load_sem, fs, fr, bs, br, ls, lr, gs, gr, xs, xr, es, er, hs, hr, ws, wr, vs, ps, pr, rs, rr,
):
    me = lax.axis_index("adapter")
    z = lax.axis_index("tensor")
    core = lax.rem(me, NC)
    x = lax.rem(lax.div(me, NC), NX)
    y = lax.div(me, NC * NX)
    mine_q = lax.rem(z, 4)
    rows, cols = out_ref.shape
    slots = GROUPS * CAP
    kcols = xb.shape[-1]
    quarter = rows // 4
    wblk = w_hbm.shape[0]
    hcols = cols // 2

    def part_of(g):
        return pl.ds(g * hcols, hcols)

    def dev(yy, xx, cc):
        return (yy * NX + xx) * NC + cc

    def remote(src, dst, ssem, rsem, a, t):
        return pltpu.make_async_remote_copy(
            src_ref=src, dst_ref=dst, send_sem=ssem, recv_sem=rsem,
            device_id=(a, t), device_id_type=MESH)

    load_x = pltpu.make_async_copy(
        att.at[:, pl.ds(pl.multiple_of(z * cols, cols), cols)], xz, load_sem.at[0])
    load_x.start()
    load_down = pltpu.make_async_copy(down_hbm, down, load_sem.at[1])
    load_down.start()
    load_up = pltpu.make_async_copy(up_hbm, up, load_sem.at[2])
    load_up.start()
    load_res = pltpu.make_async_copy(res_hbm, res, load_sem.at[3])
    load_res.start()

    barrier = pltpu.get_barrier_semaphore()

    def greet(d, _):
        pl.semaphore_signal(barrier, inc=1, device_id=(lax.rem(me + d, GROUPS), z),
                            device_id_type=MESH)
        return 0

    lax.fori_loop(1, GROUPS, greet, 0)

    def greet_z(d, _):
        pl.semaphore_signal(barrier, inc=1, device_id=(me, lax.rem(z + d, nz)),
                            device_id_type=MESH)
        return 0

    lax.fori_loop(1, nz, greet_z, 0)

    pl.semaphore_wait(barrier, GROUPS - 1 + nz - 1)

    def block(ref, i):
        return ref.at[pl.ds(pl.multiple_of(i * CAP, CAP), CAP), :]

    def fwd_copy(to):
        return remote(block(fwd, to), block(got, me), fs.at[to], fr.at[me], to, z)

    def x_copy(dy, dc):
        yd = lax.rem(y + dy, NY)
        cd = lax.rem(core + dc, NC)
        src = att.at[pl.ds(pl.multiple_of(mine_q * quarter, quarter), quarter),
                     pl.ds(pl.multiple_of((yd * NC + cd) * kcols, kcols), kcols)]
        dst = xb.at[mine_q, dc, y]
        if dy == 0 and dc == 0:
            return pltpu.make_async_copy(src, dst, xr.at[dc, y])
        return remote(src, dst, xs.at[dc, dy], xr.at[dc, y], dev(yd, x, cd), z)

    def send_x():
        for dy in (2, 1, 3, 0):
            for dc in range(NC):
                x_copy(dy, dc).start()

    send_x()
    half = lax.div(x, 2)
    spot = lax.rem(x, 2) * NC + core
    hblk = wblk // 2

    def w_part(p, h, g):
        return wg.at[pl.ds(pl.multiple_of(p * wblk + h * hblk, hblk), hblk), part_of(g)]

    def w_copy(dx, h, g):
        return remote(w_hbm.at[pl.ds(h * hblk, hblk), part_of(g)], w_part(spot, h, g),
                      ws.at[dx, h, g], wr.at[spot, h, g], dev(y, lax.rem(x + dx, NX), half), z)

    def send_w(g):
        for i in range(2):
            w_copy(1, i, g).start()
            w_copy(3, 1 - i, g).start()

        @pl.when(half == core)
        def _():
            for h in range(2):
                pltpu.make_async_copy(w_hbm.at[pl.ds(h * hblk, hblk), part_of(g)],
                                      w_part(spot, h, g), wr.at[spot, h, g]).start()

        @pl.when(half != core)
        def _():
            for h in range(2):
                w_copy(0, h, g).start()

    ahead = lax.rem(x - 2 * core + NX, NX)
    near = lax.rem(ahead + 1, 2)
    side = 1 - lax.rem(lax.div(ahead + 1, 2), 2)

    def w_pass(c, g):
        part = w_part(near * NC + c, side, g)
        return remote(part, part, vs.at[c, g], wr.at[near * NC + c, side, g],
                      dev(y, lax.rem(x + 1 + 2 * side, NX), core), z)

    def w_arrived(p, h, g):
        part = w_part(p, h, g)
        pltpu.make_async_copy(part, part, wr.at[p, h, g]).wait()

    def pass_on(g):
        for c in range(NC):
            w_arrived(near * NC + c, side, g)
            w_pass(c, g).start()

    def w_ready(g):
        for c in range(NC):
            w_arrived(near * NC + c, 1 - side, g)
            w_arrived((1 - near) * NC + c, 0, g)
            w_arrived((1 - near) * NC + c, 1, g)

    right, left = lax.rem(z + 1, nz), lax.rem(z + nz - 1, nz)
    left_q, right_q, far_q = lax.rem(mine_q + 3, 4), lax.rem(mine_q + 1, 4), lax.rem(mine_q + 2, 4)

    def e_copy(way, rel, yy):
        ref = xb.at[mine_q, rel, yy]
        return remote(ref, ref, es.at[way, rel, yy], er.at[way, rel, yy], me, (right, left)[way])

    def h_copy(way, yy):
        ref = xb.at[(left_q, right_q)[way], way, yy]
        return remote(ref, ref, hs.at[way, yy], hr.at[way, yy], me, (right, left)[way])

    def arrived(q, rel, yy, sem):
        ref = xb.at[q, rel, yy]
        pltpu.make_async_copy(ref, ref, sem).wait()

    def share(i, _):
        yy = lax.rem(i, NY)
        rel = lax.div(i, NY)
        arrived(mine_q, rel, yy, xr.at[rel, yy])
        e_copy(0, rel, yy).start()
        e_copy(1, rel, yy).start()
        return 0

    def share_on(yy, _):
        for way in range(2):
            arrived((left_q, right_q)[way], way, yy, er.at[way, way, yy])
            h_copy(way, yy).start()
        return 0

    send_w(0)
    ids = idx_ref[...]
    owner = lax.shift_right_logical(ids, 4)
    local = lax.bitwise_and(ids, CAP - 1)
    hits = (iota((GROUPS, rows), 0) == owner).astype(bf16)
    earlier = (iota((rows, rows), 0) < iota((rows, rows), 1)).astype(bf16)
    before = jnp.dot(hits, earlier, preferred_element_type=f32)
    position = jnp.sum(before * hits.astype(f32), axis=0, keepdims=True)
    target = owner.astype(f32) * CAP + position
    eye = iota((rows, rows), 0) == iota((rows, rows), 1)
    target_col = jnp.sum(jnp.where(eye, target, 0.0), axis=1, keepdims=True)
    local_col = jnp.sum(jnp.where(eye, local.astype(f32), 0.0), axis=1, keepdims=True)
    placing = (iota((slots, rows), 0) == target.astype(i32)).astype(bf16)

    load_x.wait()
    fwd[:, :cols] = jnp.dot(placing, xz[...], preferred_element_type=f32).astype(bf16)
    fwd[:, cols:] = jnp.dot(
        placing, jnp.broadcast_to(local_col, (rows, META)).astype(bf16),
        preferred_element_type=f32).astype(bf16)

    pass_on(0)
    for dy, dx, dc in FAR_FIRST:
        fwd_copy(dev(lax.rem(y + dy, NY), lax.rem(x + dx, NX), lax.rem(core + dc, NC))).start()
    pltpu.make_async_copy(block(fwd, me), block(got, me), fr.at[me]).start()

    lax.fori_loop(0, NY * NC, share, 0)
    def base(k, g):
        place = pl.ds(pl.multiple_of(k * quarter, quarter), quarter)
        tile = min(256, hcols)

        def one(n, _):
            at = pl.ds(pl.multiple_of(g * hcols + n * tile, tile), tile)
            r = jnp.dot(xb[k].reshape(NC * NY * quarter, kcols), wg[:, at],
                        preferred_element_type=f32)
            r = r.reshape(NC, NY, quarter, tile)
            keep[:, place, at] = r[0]
            sib_out[:, place, at] = r[1].astype(bf16)
            return 0

        lax.fori_loop(0, hcols // tile, one, 0)

    def from_sides(yy, _):
        arrived(left_q, 1, yy, er.at[0, 1, yy])
        arrived(right_q, 0, yy, er.at[1, 0, yy])
        return 0

    def from_far(yy, _):
        for way in range(2):
            arrived(far_q, way, yy, hr.at[way, yy])
        return 0

    def pair_copy(yy, g):
        return remote(sib_out.at[yy, :, part_of(g)], sib_in.at[yy, :, part_of(g)], ps.at[yy, g],
                      pr.at[yy, g], dev(y, x, 1 - core), z)

    def sum_copy(dy, g):
        yd = lax.rem(y + dy, NY)
        return remote(sum_out.at[dy, :, part_of(g)], sum_in.at[dy, :, part_of(g)], rs.at[dy, g],
                      rr.at[dy, g], dev(yd, x, core), z)

    def project_base(g):
        w_ready(g)
        base(mine_q, g)
        if g == 0:
            lax.fori_loop(0, NY, from_sides, 0)
        base(left_q, g)
        base(right_q, g)

    def project_far(g):
        if g == 0:
            lax.fori_loop(0, NY, from_far, 0)
        base(far_q, g)
        for dy in (2, 1, 3, 0):
            pair_copy(lax.rem(y + dy, NY), g).start()

    def send_sum(g):
        at = slice(g * hcols, (g + 1) * hcols)
        for dy in (2, 1, 3, 0):
            yd = lax.rem(y + dy, NY)
            ref = sib_in.at[yd, :, part_of(g)]
            pltpu.make_async_copy(ref, ref, pr.at[yd, g]).wait()
            if dy == 0:
                keep[yd, :, at] = keep[yd, :, at] + sib_in[yd, :, at].astype(f32)
            else:
                sum_out[dy, :, at] = (keep[yd, :, at] + sib_in[yd, :, at].astype(f32)).astype(bf16)
                sum_copy(dy, g).start()

    lax.fori_loop(0, NY, share_on, 0)
    project_base(0)

    def got_fwd(s, _):
        pltpu.make_async_copy(block(got, s), block(got, s), fr.at[s]).wait()
        return 0

    lax.fori_loop(0, GROUPS, got_fwd, 0)
    send_w(1)
    load_down.wait()
    lane = iota((slots, 128), 1)
    mine = got[:, cols:].astype(f32) - (lane >= 64).astype(f32)
    acc = jnp.zeros((slots, 128), f32)
    for t in range(4):
        projected = lax.dot_general(
            got[:, :cols], down[t * 256:(t + 1) * 256, :], (((1,), (1,)), ((), ())),
            preferred_element_type=f32)
        for u in range(2):
            acc += jnp.where(mine == 2.0 * (2 * t + u), projected[:, u * 128:(u + 1) * 128], 0.0)
    acc = acc + pltpu.roll(acc, 64, 1)
    first = iota((slots // 2, 128), 1) < 64
    low_own[...] = jnp.where(first, acc[:slots // 2], acc[slots // 2:]).reshape(low_own.shape)

    def low_send(d, _):
        to = lax.rem(z + d, nz)
        remote(low_own.at[to], low_in.at[z], ls.at[to], lr.at[z], me, to).start()
        return 0

    lax.fori_loop(1, nz, low_send, 0)
    project_far(0)

    def low_got(d, total):
        s = lax.rem(z + d, nz)
        pltpu.make_async_copy(low_in.at[s], low_in.at[s], lr.at[s]).wait()
        return total + low_in[s]

    low_sum[...] = lax.fori_loop(1, nz, low_got, low_own[z]).astype(bf16)

    def low_spread(d, _):
        to = lax.rem(z + d, nz)
        remote(low_sum, low_all.at[z], gs.at[to], gr.at[z], me, to).start()
        return 0

    lax.fori_loop(1, nz, low_spread, 0)
    low_all[z] = low_sum[...]

    def up_and_back():
        def low_here(d, _):
            s = lax.rem(z + d, nz)
            pltpu.make_async_copy(low_all.at[s], low_all.at[s], gr.at[s]).wait()
            return 0

        lax.fori_loop(1, nz, low_here, 0)
        load_up.wait()
        packed = low_all[...].reshape(slots // 2, 128).astype(f32)
        turned = pltpu.roll(packed, 64, 1)
        low = jnp.concatenate(
            [jnp.where(first, packed, turned), jnp.where(first, turned, packed)], axis=0)
        for j in range(8):
            spread[:, j * 128:(j + 1) * 128] = jnp.where(mine == 2.0 * j, low, 0.0).astype(bf16)
        tile = min(256, cols)

        def up_tile(n, _):
            at = pl.ds(pl.multiple_of(n * tile, tile), tile)
            delta[:, at] = (jnp.dot(spread[...], up[:, at], preferred_element_type=f32)
                            * adapter_scale).astype(bf16)
            return 0

        lax.fori_loop(0, cols // tile, up_tile, 0)

        for dy, dx, dc in FAR_FIRST:
            to = dev(lax.rem(y + dy, NY), lax.rem(x + dx, NX), lax.rem(core + dc, NC))
            remote(block(delta, to), block(back, me), bs.at[to], br.at[me], to, z).start()
        pltpu.make_async_copy(block(delta, me), block(back, me), br.at[me]).start()

    pass_on(1)
    send_sum(0)
    up_and_back()
    project_base(1)
    project_far(1)
    send_sum(1)

    load_res.wait()
    for g in range(2):
        for dy in (1, 3, 2):
            ref = sum_in.at[dy, :, part_of(g)]
            pltpu.make_async_copy(ref, ref, rr.at[dy, g]).wait()
    total = (res[...].astype(f32) + keep[y] + sum_in[1].astype(f32) + sum_in[2].astype(f32)
             + sum_in[3].astype(f32))
    homing = (iota((rows, slots), 1) == target_col.astype(i32)).astype(bf16)

    def got_back(s, _):
        pltpu.make_async_copy(block(back, s), block(back, s), br.at[s]).wait()
        return 0

    lax.fori_loop(0, GROUPS, got_back, 0)
    total = total + jnp.dot(homing, back[...], preferred_element_type=f32)
    out_ref[...] = total.astype(bf16)

    def sent(d, _):
        to = lax.rem(me + d, GROUPS)
        remote(block(fwd, to), block(got, me), fs.at[to], fr.at[me], to, z).wait_send()
        remote(block(delta, to), block(back, me), bs.at[to], br.at[me], to, z).wait_send()
        return 0

    lax.fori_loop(1, GROUPS, sent, 0)

    def sent_z(d, _):
        to = lax.rem(z + d, nz)
        remote(low_own.at[to], low_in.at[z], ls.at[to], lr.at[z], me, to).wait_send()
        remote(low_sum, low_all.at[z], gs.at[to], gr.at[z], me, to).wait_send()
        return 0

    lax.fori_loop(1, nz, sent_z, 0)
    for dy in range(NY):
        for dc in range(NC):
            if dy or dc:
                x_copy(dy, dc).wait_send()
            for way in range(2):
                e_copy(way, dc, dy).wait_send()
        for way in range(2):
            h_copy(way, dy).wait_send()
    for g in range(2):
        for dx in (1, 3):
            for h in range(2):
                w_copy(dx, h, g).wait_send()
        for dx in (1, 2, 3):
            sum_copy(dx, g).wait_send()
        for c in range(NC):
            w_pass(c, g).wait_send()
        for dy in range(NY):
            pair_copy(dy, g).wait_send()

    @pl.when(half != core)
    def _():
        for g in range(2):
            for h in range(2):
                w_copy(0, h, g).wait_send()


def per_device(
    attended, residual, output_matrix, adapter_down_weight, adapter_up_weight, request_adapter_index
):
    nz = lax.axis_size("tensor")
    rows, width = attended.shape
    cols = width // nz
    kcols = width // (NY * NC)
    adapters, rank, unused_value = adapter_down_weight.shape
    slots = GROUPS * CAP
    wide = adapters * rank
    quarter = rows // 4
    dma = pltpu.SemaphoreType.DMA
    anyspace = pl.BlockSpec(memory_space=pl.ANY)
    vmem = pl.BlockSpec(memory_space=pltpu.VMEM)
    return pl.pallas_call(
        functools.partial(kernel, nz),
        out_shape=jax.ShapeDtypeStruct((rows, cols), bf16),
        in_specs=[vmem] + [anyspace] * 5,
        out_specs=vmem,
        scratch_shapes=[
            pltpu.VMEM((rows, cols), bf16),
            pltpu.VMEM((rows, cols), bf16),
            pltpu.VMEM((wide, cols), bf16),
            pltpu.VMEM((wide, cols), bf16),
            pltpu.VMEM((slots, cols + META), bf16),
            pltpu.VMEM((slots, cols + META), bf16),
            pltpu.VMEM((nz, slots // 2 // nz, 128), f32),
            pltpu.VMEM((nz, slots // 2 // nz, 128), f32),
            pltpu.VMEM((slots // 2 // nz, 128), bf16),
            pltpu.VMEM((nz, slots // 2 // nz, 128), bf16),
            pltpu.VMEM((slots, wide), bf16),
            pltpu.VMEM((slots, cols), bf16),
            pltpu.VMEM((slots, cols), bf16),
            pltpu.VMEM((4, NC, NY, quarter, kcols), bf16),
            pltpu.VMEM((kcols, cols), bf16),
            pltpu.VMEM((NY, rows, cols), f32),
            pltpu.VMEM((NY, rows, cols), bf16),
            pltpu.VMEM((NY, rows, cols), bf16),
            pltpu.VMEM((NY, rows, cols), bf16),
            pltpu.VMEM((NY, rows, cols), bf16),
            dma((4,)),
            dma((GROUPS,)), dma((GROUPS,)),
            dma((GROUPS,)), dma((GROUPS,)),
            dma((nz,)), dma((nz,)),
            dma((nz,)), dma((nz,)),
            dma((NC, NY)), dma((NC, NY)),
            dma((2, NC, NY)), dma((2, NC, NY)),
            dma((2, NY)), dma((2, NY)),
            dma((4, 2, 2)), dma((4, 2, 2)), dma((NC, 2)),
            dma((NY, 2)), dma((NY, 2)),
            dma((NY, 2)), dma((NY, 2)),
        ],
        compiler_params=pltpu.CompilerParams(
            collective_id=0, has_side_effects=True, vmem_limit_bytes=60 * 1024 * 1024),
    )(
        request_adapter_index.reshape(1, rows), attended, residual, output_matrix,
        adapter_down_weight.reshape(wide, cols), adapter_up_weight.reshape(wide, cols),
    )


def solution(mesh):
    return jax.shard_map(
        per_device,
        mesh=mesh,
        in_specs=(
            P("adapter", None),
            P("adapter", "tensor"),
            P("adapter", "tensor"),
            P("adapter", None, "tensor"),
            P("adapter", None, "tensor"),
            P("adapter"),
        ),
        out_specs=P("adapter", "tensor"),
        check_vma=False,
    )
```
